256 devices in a mesh: gx: 16 (over x, y), gy: 4 (over z_hi), gz: 4 (over z_lo, core).
Axes of the slice: x: 4, y: 4, z: 8 (z_hi: 4, z_lo: 2; z = z_hi * 2 + z_lo), core: 2. Of those that a mesh axis runs over, the one named last changes fastest.
Arguments:
- tokens: bfloat16 [4096, 4096], P(('gz', 'gx'), 'gy'), may hold values from -6 to 6
- gate_weight: bfloat16 [4096, 10240], P(('gy', 'gz'), 'gx'), may hold values from -0.09375 to 0.09375
- up_weight: bfloat16 [4096, 10240], P(('gy', 'gz'), 'gx'), may hold values from -0.09375 to 0.09375
- down_weight: bfloat16 [10240, 4096], P('gx', ('gy', 'gz')), may hold values from -0.0625 to 0.0625
- out_cotangent: bfloat16 [4096, 4096], P(('gz', 'gx'), 'gy'), may hold values from -6 to 6
Outputs:
- output: bfloat16 [4096, 4096], P(('gz', 'gx'), 'gy')
- input_grad: bfloat16 [4096, 4096], P(('gz', 'gx'), 'gy')
- gate_weight_grad: bfloat16 [4096, 10240], P(('gy', 'gz'), 'gx')
- up_weight_grad: bfloat16 [4096, 10240], P(('gy', 'gz'), 'gx')
- down_weight_grad: bfloat16 [10240, 4096], P('gx', ('gy', 'gz'))
The draws below stay inside these ranges and needn't reach their ends.
All inputs are finite; a program needn't handle non-finite values.
Results may differ from the reference program's by a relative error of at most 0.029.
Values may be sent and summed in bfloat16 or wider, within the bound.
No kernel may reach another device: no remote copies, remote signals or barrier semaphores. Data moves between devices by JAX's collectives and lax.ppermute only.
A program may use at most 64 MiB of HBM per device.

```python
import math
import jax
import jax.numpy as jnp
from jax import lax

D = 4096
FF = 10240
TOKENS = 4096
N_GY = 4
N_GZ = 4


def block_levels(own_key, shape, pieces, smallest, largest):
    factor_of = 1.0
    for dim, blocks in pieces:
        steps = jax.random.uniform(jax.random.fold_in(jax.random.fold_in(own_key, 6), dim), (blocks,), jnp.float32, smallest / len(pieces), largest / len(pieces))
        factor_of = factor_of * jnp.repeat(jnp.exp(steps), shape[dim] // blocks).reshape((-1,) + (1,) * (len(shape) - 1 - dim))
    return factor_of


def normal_values(key, extent, spread, reach, shards=(), kind=jnp.bfloat16):
    array = jax.random.normal(key, extent, jnp.float32) * spread
    if len(shards) > 0:
        array = block_levels(key, extent, shards, -0.22, 0.18) * array
    return jnp.clip(array, min=-reach, max=reach).astype(kind)


def setup_inputs(seed: int = 0) -> dict:
    splits = jax.random.split(jax.random.key(seed), 6)
    tokens = normal_values(splits[0], (TOKENS, D), 1.0, 6.0, ((0, 64), (1, 4)))
    gate_weight = normal_values(splits[1], (D, FF), D ** -0.5, 0.09375, ((0, 16), (1, 16)))
    up_weight = normal_values(splits[2], (D, FF), D ** -0.5, 0.09375, ((0, 16), (1, 16)))
    down_weight = normal_values(splits[3], (FF, D), FF ** -0.5, 0.0625, ((0, 16), (1, 16)))
    out_cotangent = normal_values(splits[4], (TOKENS, D), 1.0, 6.0, ((0, 64), (1, 4)))
    return {"tokens": tokens, "gate_weight": gate_weight, "up_weight": up_weight, "down_weight": down_weight, "out_cotangent": out_cotangent}


gelu_scale = math.sqrt(2.0 / math.pi)
cubic_coef = 0.044715

def gelu_pair(value):
    inner = gelu_scale * (value + cubic_coef * value * value * value)
    tangent = jnp.tanh(inner)
    activation = 0.5 * value * (1.0 + tangent)
    slope = 0.5 * (1.0 + tangent) + 0.5 * value * (1.0 - tangent * tangent) * gelu_scale * (1.0 + 3.0 * cubic_coef * value * value)
    return (activation, slope)

def blocked(left, right, count):
    width = left.shape[1] // count
    total = jnp.zeros((left.shape[0], right.shape[1]), jnp.float32)
    for position in range(count):
        term = jnp.dot(left[:, position * width:(position + 1) * width], right[position * width:(position + 1) * width, :], preferred_element_type=jnp.float32)
        total = total + lax.optimization_barrier(term.astype(jnp.bfloat16)).astype(jnp.float32)
    return total

def reference(tokens, gate_weight, up_weight, down_weight, out_cotangent):
    gate = blocked(tokens, gate_weight, N_GY)
    up_value = blocked(tokens, up_weight, N_GY)
    activation, slope = gelu_pair(gate)
    hidden = (activation * up_value).astype(jnp.bfloat16)
    output = jnp.dot(hidden, down_weight, preferred_element_type=jnp.float32).astype(jnp.bfloat16)
    hidden_grad = blocked(out_cotangent, down_weight.T, N_GY)
    gate_grad = (hidden_grad * up_value * slope).astype(jnp.bfloat16)
    up_grad = (hidden_grad * activation).astype(jnp.bfloat16)
    input_grad = (jnp.dot(gate_grad, gate_weight.T, preferred_element_type=jnp.float32) + jnp.dot(up_grad, up_weight.T, preferred_element_type=jnp.float32)).astype(jnp.bfloat16)
    down_weight_grad = blocked(hidden.T, out_cotangent, N_GZ).astype(jnp.bfloat16)
    gate_weight_grad = blocked(tokens.T, gate_grad, N_GZ).astype(jnp.bfloat16)
    up_weight_grad = blocked(tokens.T, up_grad, N_GZ).astype(jnp.bfloat16)
    return (output, input_grad, gate_weight_grad, up_weight_grad, down_weight_grad)
```

```python
import math

import jax
import jax.numpy as jnp
from jax import lax
from jax.experimental import pallas as pl
from jax.experimental.pallas import tpu as pltpu
from jax.sharding import Mesh
from jax.sharding import PartitionSpec as P

gelu_scale = math.sqrt(2.0 / math.pi)
cubic_coef = 0.044715
F32, BF16 = jnp.float32, jnp.bfloat16
Z = ("zh", "zl")
NZ = 8
VMEM = 40 * 1024 * 1024


def gelu_pair(value):
    inner = gelu_scale * (value + cubic_coef * value * value * value)
    tangent = jnp.tanh(inner)
    activation = 0.5 * value * (1.0 + tangent)
    slope = 0.5 * (1.0 + tangent) + 0.5 * value * (1.0 - tangent * tangent) * gelu_scale * (
        1.0 + 3.0 * cubic_coef * value * value
    )
    return (activation, slope)


def dot(left, right, contract):
    return lax.dot_general(left, right, ((contract[0:1], contract[1:2]), ((), ())), preferred_element_type=F32)


def params(steps=1):
    return pltpu.CompilerParams(vmem_limit_bytes=VMEM, dimension_semantics=("arbitrary",) * steps)


def cost(flops, moved):
    return pl.CostEstimate(flops=flops, bytes_accessed=moved, transcendentals=0)


def gate_up_kernel(weights, inputs, hidden, activation, slope_up, slope_act, total):
    step = pl.program_id(0)
    part = dot(weights[0], inputs[...], (1, 1))

    @pl.when(step == 0)
    def _():
        total[...] = part

    @pl.when(step > 0)
    def _():
        total[...] += part

    @pl.when(step == pl.num_programs(0) - 1)
    def _():
        half = total.shape[0] // 2
        up_value = total[half:, :]
        act, slope = gelu_pair(total[:half, :])
        hidden[...] = (act * up_value).astype(BF16)
        activation[...] = act
        slope_up[...] = up_value
        slope_act[...] = slope


def gate_up(weights, inputs):
    steps, rows, width = weights.shape
    count = inputs.shape[0]
    half = rows // 2
    whole = pl.BlockSpec((half, count), lambda i: (0, 0))
    return pl.pallas_call(
        gate_up_kernel,
        grid=(steps,),
        in_specs=[
            pl.BlockSpec((1, rows, width), lambda i: (i, 0, 0)),
            pl.BlockSpec((count, width), lambda i: (0, i)),
        ],
        out_specs=[whole] * 4,
        out_shape=[jax.ShapeDtypeStruct((half, count), BF16)] + [jax.ShapeDtypeStruct((half, count), F32)] * 3,
        scratch_shapes=[pltpu.VMEM((rows, count), F32)],
        compiler_params=params(),
        cost_estimate=cost(2 * steps * rows * width * count, 12_000_000),
    )(weights, inputs)


def hidden_grad_kernel(weights, cotangent, activation, up_value, slope, grads, total):
    step = pl.program_id(0)
    part = dot(weights[0], cotangent[...], (1, 1))

    @pl.when(step == 0)
    def _():
        total[...] = part

    @pl.when(step > 0)
    def _():
        total[...] += part

    @pl.when(step == pl.num_programs(0) - 1)
    def _():
        half = total.shape[0]
        hidden_grad = total[...]
        grads[:half, :] = (hidden_grad * up_value[...] * slope[...]).astype(BF16)
        grads[half:, :] = (hidden_grad * activation[...]).astype(BF16)


def hidden_grad(weights, cotangent, activation, up_value, slope):
    steps, rows, width = weights.shape
    count = cotangent.shape[0]
    whole = pl.BlockSpec((rows, count), lambda i: (0, 0))
    return pl.pallas_call(
        hidden_grad_kernel,
        grid=(steps,),
        in_specs=[
            pl.BlockSpec((1, rows, width), lambda i: (i, 0, 0)),
            pl.BlockSpec((count, width), lambda i: (0, i)),
            whole,
            whole,
            whole,
        ],
        out_specs=pl.BlockSpec((2 * rows, count), lambda i: (0, 0)),
        out_shape=jax.ShapeDtypeStruct((2 * rows, count), BF16),
        scratch_shapes=[pltpu.VMEM((rows, count), F32)],
        compiler_params=params(),
        cost_estimate=cost(2 * steps * rows * width * count, 9_000_000),
    )(weights, cotangent, activation, up_value, slope)


def weight_grad_kernel(left, right, out):
    out[0] = dot(left[...], right[...], (1, 0)).astype(BF16)


def weight_grad(left, right, steps):
    rows, count = left.shape
    width = right.shape[1] // steps
    return pl.pallas_call(
        weight_grad_kernel,
        grid=(steps,),
        in_specs=[
            pl.BlockSpec((rows, count), lambda i: (0, 0)),
            pl.BlockSpec((count, width), lambda i: (0, i)),
        ],
        out_specs=pl.BlockSpec((1, rows, width), lambda i: (i, 0, 0)),
        out_shape=jax.ShapeDtypeStruct((steps, rows, width), BF16),
        compiler_params=params(),
        cost_estimate=cost(2 * steps * rows * width * count, 10_000_000),
    )(left, right)


def token_product_kernel(left, weights, out):
    out[...] = dot(left[...], weights[0], (0, 0)).astype(BF16)


def token_product(left, weights):
    steps, rows, width = weights.shape
    count = left.shape[1]
    return pl.pallas_call(
        token_product_kernel,
        grid=(steps,),
        in_specs=[
            pl.BlockSpec((rows, count), lambda i: (0, 0)),
            pl.BlockSpec((1, rows, width), lambda i: (i, 0, 0)),
        ],
        out_specs=pl.BlockSpec((count, width), lambda i: (0, i)),
        out_shape=jax.ShapeDtypeStruct((count, steps * width), BF16),
        compiler_params=params(),
        cost_estimate=cost(2 * steps * rows * width * count, 10_000_000),
    )(left, weights)


def shift(array, axis, by, size=4):
    return lax.ppermute(array, axis, [(i, (i + by) % size) for i in range(size)])


def ring_gather(block, axis):
    back, ahead = shift(block, axis, 1), shift(block, axis, -1)
    half = block.shape[-1] // 2
    far = jnp.concatenate(
        [shift(back[..., :half], axis, 1), shift(ahead[..., half:], axis, -1)], axis=-1
    )
    return [block, back, far, ahead]


def add(*terms):
    return sum(t.astype(F32) for t in terms).astype(BF16)


def ring_scatter(blocks, axis):
    own, back, far, ahead = blocks
    half = own.shape[-1] // 2
    left, right = shift(far[..., :half], axis, -1), shift(far[..., half:], axis, 1)
    back = jnp.concatenate([add(back[..., :half], left), back[..., half:]], axis=-1)
    ahead = jnp.concatenate([ahead[..., :half], add(ahead[..., half:], right)], axis=-1)
    return add(own, shift(back, axis, -1), shift(ahead, axis, 1))


def gather_tokens(block, first, second, order):
    inner = jnp.stack(ring_gather(block, first), 0)
    outer = jnp.stack(ring_gather(inner, second), order)
    own = outer.reshape(-1, block.shape[-1])
    other = shift(own, "c", 1, 2)
    return jnp.concatenate([own, other], 0)


def scatter_tokens(partial, first, order):
    half = partial.shape[0] // 2
    own = add(partial[:half], shift(partial[half:], "c", 1, 2))
    own = own.reshape(4, 4, half // 16, -1)
    pieces = [lax.index_in_dim(own, k, order, keepdims=False) for k in range(4)]
    inner = ring_scatter(pieces, first)
    second = "x" if first == "y" else "y"
    block = ring_scatter([inner[k] for k in range(4)], second)
    return lax.all_to_all(block, "zh", 1, 0, tiled=True)


def local(tokens, gate_weight, up_weight, down_weight, out_cotangent):
    weights = jnp.stack([gate_weight.T, up_weight.T, down_weight], 0)
    weights = lax.all_to_all(weights, "c", 1, 2, tiled=True)
    gate_up_rows = lax.all_gather(weights[:2], Z, axis=0).reshape(NZ, -1, weights.shape[-1])
    down_rows = lax.all_gather(weights[2], Z, axis=0)

    both = jnp.stack([tokens, out_cotangent], 0)
    both = lax.all_to_all(both, "zh", 1, 2, tiled=True)
    inputs = gather_tokens(both[0], "x", "y", 0)
    cotangent = gather_tokens(both[1], "y", "x", 1)

    hidden, activation, up_value, slope = gate_up(gate_up_rows, inputs)
    down_partial = weight_grad(hidden, cotangent, NZ)
    grads = hidden_grad(down_rows, cotangent, activation, up_value, slope)
    both_partial = weight_grad(grads, inputs, NZ)
    input_partial = token_product(grads, gate_up_rows)
    out_partial = token_product(hidden, down_rows)

    down_total = lax.psum_scatter(down_partial, Z, scatter_dimension=0, tiled=False)
    both_total = lax.psum_scatter(both_partial, Z, scatter_dimension=0, tiled=False)
    output = scatter_tokens(out_partial, "y", 0)
    input_grad = scatter_tokens(input_partial, "x", 1)

    half = down_total.shape[0]
    totals = jnp.stack([both_total[:half], both_total[half:], down_total], 0)
    totals = lax.all_to_all(totals, "c", 2, 1, tiled=True)
    return (output, input_grad, totals[0].T, totals[1].T, totals[2])


def solution(mesh):
    fine = Mesh(mesh.devices.reshape(4, 4, 4, 2, 2), ("x", "y", "zh", "zl", "c"))
    token_spec = P(("zl", "c", "x", "y"), "zh")
    in_spec = P(("zh", "zl", "c"), ("x", "y"))
    out_spec = P(("x", "y"), ("zh", "zl", "c"))
    return jax.shard_map(
        local,
        mesh=fine,
        in_specs=(token_spec, in_spec, in_spec, out_spec, token_spec),
        out_specs=(token_spec, token_spec, in_spec, in_spec, out_spec),
        check_vma=False,
    )
```

```python
import math

import jax
import jax.numpy as jnp
from jax import lax
from jax.sharding import Mesh
from jax.sharding import PartitionSpec as P

gelu_scale = math.sqrt(2.0 / math.pi)
cubic_coef = 0.044715
F32, BF16 = jnp.float32, jnp.bfloat16
Z = ("zh", "zl")
NZ = 8


def gelu_pair(value):
    inner = gelu_scale * (value + cubic_coef * value * value * value)
    tangent = jnp.tanh(inner)
    activation = 0.5 * value * (1.0 + tangent)
    slope = 0.5 * (1.0 + tangent) + 0.5 * value * (1.0 - tangent * tangent) * gelu_scale * (
        1.0 + 3.0 * cubic_coef * value * value
    )
    return (activation, slope)


def product(left, right, left_dim, right_dim):
    return lax.dot_general(
        left, right, (((left_dim,), (right_dim,)), ((), ())), preferred_element_type=F32
    ).astype(BF16)


def shift(array, axis, by, size=4):
    return lax.ppermute(array, axis, [(i, (i + by) % size) for i in range(size)])


def add(*terms):
    return sum(t.astype(F32) for t in terms).astype(BF16)


def core_sum(part):
    return part.astype(F32) + shift(part, "c", 1, 2).astype(F32)


def ring_scatter_z(partial, z):
    rows, columns = partial.shape[0], partial.shape[1] // NZ
    half = rows // 2

    def take(ahead, offset=0, count=rows):
        start = (jnp.int32(offset), lax.rem(z + ahead, NZ) * columns)
        return lax.dynamic_slice(partial, start, (count, columns))

    def send(pair):
        return shift(pair[0], Z, 1, NZ), shift(pair[1], Z, -1, NZ)

    up, down = send((yield take(4, 0, half), take(4, half, half)))
    up = jnp.concatenate([add(take(3, 0, half), up), take(3, half, half)], 0)
    down = jnp.concatenate([take(5, 0, half), add(take(5, half, half), down)], 0)
    for step in (2, 1):
        up, down = send((yield up, down))
        up, down = add(take(step), up), add(take(NZ - step), down)
    up, down = send((yield up, down))
    yield add(take(0), up, down)


def ring_gather_z(block, z):
    rows, columns = block.shape
    half = rows // 2
    out = jnp.zeros((rows, NZ * columns), block.dtype)

    def put(out, piece, back, offset=0):
        start = (jnp.int32(offset), lax.rem(z + NZ - back, NZ) * columns)
        return lax.dynamic_update_slice(out, piece, start)

    out = put(out, block, 0)
    back = ahead = block
    for step in (1, 2, 3):
        back, ahead = shift(back, Z, 1, NZ), shift(ahead, Z, -1, NZ)
        out = put(put(out, back, step), ahead, NZ - step)
    out = put(out, shift(back[:half], Z, 1, NZ), 4)
    return put(out, shift(ahead[half:], Z, -1, NZ), 4, half)


def ring_gather(block, axis, dim):
    me = lax.axis_index(axis)
    back, ahead = shift(block, axis, 1), shift(block, axis, -1)
    if block.ndim == 2:
        far = [(0, shift(block, axis, 2))]
    else:
        far = [(0, shift(back[:2], axis, 1)), (2, shift(ahead[2:], axis, -1))]
    out = jnp.zeros(block.shape[:dim] + (4,) + block.shape[dim:], block.dtype)
    for k, offset, piece in [(0, 0, block), (1, 0, back), (3, 0, ahead)] + [(2, o, p) for o, p in far]:
        start = [jnp.int32(0)] * out.ndim
        start[1 - dim if block.ndim == 3 else 0] = jnp.int32(offset)
        start[dim] = lax.rem(me + 4 - k, 4)
        out = lax.dynamic_update_slice(out, jnp.expand_dims(piece, dim), start)
    return out


def gather_tokens(block, first, second):
    out = ring_gather(ring_gather(block, first, 0), second, 1 if second == "y" else 0)
    return out.reshape(-1, block.shape[-1])


def scatter_start(block, axis, dim=0):
    me = lax.axis_index(axis)

    def entry(k):
        return lax.dynamic_index_in_dim(block, lax.rem(me + 4 - k, 4), dim, keepdims=False)

    return [entry(0)] + [shift(entry(k), axis, -k) for k in (1, 2, 3)]


def after(array, *others):
    return lax.optimization_barrier((array, *others))[0]


def collect_tokens(*arrays):
    count = len(arrays)
    block = jnp.stack([a.reshape(2, 16, 4, 2, 256) for a in arrays], 0)
    block = block.transpose(3, 1, 0, 2, 4, 5).reshape(8, count, 16, 2, 256)
    block = lax.all_to_all(block, ("zh", "c"), 0, 0, tiled=True)
    block = block.reshape(4, 2, count, 16, 2, 256).transpose(2, 0, 3, 4, 1, 5)
    return block.reshape(count, 64, 1024)


def spread_tokens(*arrays):
    block = jnp.stack([a.reshape(4, 16, 2, 2, 256) for a in arrays], 0)
    block = block.transpose(1, 4, 0, 2, 3, 5).reshape(8, len(arrays), 16, 2, 256)
    block = lax.all_to_all(block, ("zh", "c"), 0, 0, tiled=True)
    block = block.reshape(4, 2, len(arrays), 16, 2, 256).transpose(2, 1, 3, 0, 4, 5)
    return block.reshape(len(arrays), 32, 2048)


def local(tokens, gate_weight, up_weight, down_weight, out_cotangent):
    z = (lax.axis_index("zh") * 2 + lax.axis_index("zl")).astype(jnp.int32)
    width = gate_weight.shape[1]

    rows = lax.all_gather(jnp.concatenate([gate_weight, up_weight], 1), Z, axis=0, tiled=True)
    down_cols = ring_gather_z(down_weight, z)
    both = spread_tokens(tokens, out_cotangent)
    inputs = gather_tokens(both[0], "x", "y")
    cotangent = gather_tokens(both[1], "y", "x")

    hidden_grad = core_sum(product(cotangent, down_cols, 1, 1))
    total = core_sum(product(inputs, rows, 1, 0))
    gate, up_value = total[:, :width], total[:, width:]
    activation, slope = gelu_pair(gate)
    hidden = (activation * up_value).astype(BF16)
    grads = jnp.concatenate(
        [(hidden_grad * up_value * slope).astype(BF16), (hidden_grad * activation).astype(BF16)], 1
    )
    ring = ring_scatter_z(product(hidden, cotangent, 0, 0), z)
    pair = next(ring)
    weight_partial = product(inputs, after(grads, *pair), 0, 0)
    weight_grads = lax.psum_scatter(weight_partial, Z, scatter_dimension=0, tiled=True)
    output = product(after(hidden, weight_partial), down_cols, 1, 0).reshape(4, 4, 32, -1)
    input_grad = product(after(grads, weight_partial), rows, 1, 1).reshape(4, 4, 32, -1)
    output, input_grad = scatter_start(output, "x", 0), scatter_start(input_grad, "y", 1)
    pair = ring.send(pair)
    output = scatter_start(add(after(output[0], *pair), *output[1:]), "y")
    pair = ring.send(pair)
    input_grad = scatter_start(add(after(input_grad[0], *pair), *input_grad[1:]), "x")
    pair = ring.send(pair)
    output, input_grad = add(*output), add(*input_grad)
    down_weight_grad = ring.send(pair)
    output, input_grad = collect_tokens(output, input_grad)
    return (output, input_grad, weight_grads[:, :width], weight_grads[:, width:], down_weight_grad)


def solution(mesh):
    fine = Mesh(mesh.devices.reshape(4, 4, 4, 2, 2), ("x", "y", "zh", "zl", "c"))
    token_spec = P(("zl", "c", "x", "y"), "zh")
    in_spec = P(("zh", "zl", "c"), ("x", "y"))
    out_spec = P(("x", "y"), ("zh", "zl", "c"))
    return jax.shard_map(
        local,
        mesh=fine,
        in_specs=(token_spec, in_spec, in_spec, out_spec, token_spec),
        out_specs=(token_spec, token_spec, in_spec, in_spec, out_spec),
        check_vma=False,
    )
```

```python
import math

import jax
import jax.numpy as jnp
from jax import lax
from jax.sharding import Mesh
from jax.sharding import PartitionSpec as P

gelu_scale = math.sqrt(2.0 / math.pi)
cubic_coef = 0.044715
F32, BF16 = jnp.float32, jnp.bfloat16
Z = ("zh", "zl")
NZ = 8


def gelu_pair(value):
    inner = gelu_scale * (value + cubic_coef * value * value * value)
    tangent = jnp.tanh(inner)
    activation = 0.5 * value * (1.0 + tangent)
    slope = 0.5 * (1.0 + tangent) + 0.5 * value * (1.0 - tangent * tangent) * gelu_scale * (
        1.0 + 3.0 * cubic_coef * value * value
    )
    return (activation, slope)


def product(left, right, left_dim, right_dim):
    return lax.dot_general(
        left, right, (((left_dim,), (right_dim,)), ((), ())), preferred_element_type=F32
    ).astype(BF16)


def shift(array, axis, by, size=4):
    return lax.ppermute(array, axis, [(i, (i + by) % size) for i in range(size)])


def add(*terms):
    return sum(t.astype(F32) for t in terms).astype(BF16)


def core_sum(part):
    return part.astype(F32) + shift(part, "c", 1, 2).astype(F32)


def ring_scatter_z(partial, z):
    rows, columns = partial.shape[0], partial.shape[1] // NZ
    half = rows // 2

    def take(ahead, offset=0, count=rows):
        start = (jnp.int32(offset), lax.rem(z + ahead, NZ) * columns)
        return lax.dynamic_slice(partial, start, (count, columns))

    def send(pair):
        return shift(pair[0], Z, 1, NZ), shift(pair[1], Z, -1, NZ)

    up, down = send((yield take(4, 0, half), take(4, half, half)))
    up = jnp.concatenate([add(take(3, 0, half), up), take(3, half, half)], 0)
    down = jnp.concatenate([take(5, 0, half), add(take(5, half, half), down)], 0)
    for step in (2, 1):
        up, down = send((yield up, down))
        up, down = add(take(step), up), add(take(NZ - step), down)
    up, down = send((yield up, down))
    yield add(take(0), up, down)


def ring_gather_z(block, z):
    rows, columns = block.shape
    half = rows // 2
    out = jnp.zeros((rows, NZ * columns), block.dtype)

    def put(out, piece, back, offset=0):
        start = (jnp.int32(offset), lax.rem(z + NZ - back, NZ) * columns)
        return lax.dynamic_update_slice(out, piece, start)

    out = put(out, block, 0)
    back = ahead = block
    for step in (1, 2, 3):
        back, ahead = shift(back, Z, 1, NZ), shift(ahead, Z, -1, NZ)
        out = put(put(out, back, step), ahead, NZ - step)
    out = put(out, shift(back[:half], Z, 1, NZ), 4)
    return put(out, shift(ahead[half:], Z, -1, NZ), 4, half)


def gather_tokens(pair):
    x, y = lax.axis_index("x"), lax.axis_index("y")

    def put(out, piece, dim, at):
        start = [jnp.int32(0)] * out.ndim
        start[dim] = at
        return lax.dynamic_update_slice(out, jnp.expand_dims(piece, dim), start)

    inner = jnp.zeros((2, 4) + pair.shape[1:], pair.dtype)
    for k in range(4):
        inner = put(inner, shift(pair, "x", k) if k else pair, 1, lax.rem(x + 4 - k, 4))
    back, ahead = shift(inner, "y", 1), shift(inner, "y", -1)
    far = shift(back[0], "y", 1), shift(ahead[1], "y", -1)
    outs = []
    for n in range(2):
        out = jnp.zeros((4,) + inner.shape[1:], inner.dtype)
        for k, piece in enumerate((inner[n], back[n], far[n], ahead[n])):
            out = put(out, piece, 0, lax.rem(y + 4 - k, 4))
        outs.append(out.reshape(-1, pair.shape[-1]))
    return outs


def scatter_start(block, axis, dim=0):
    me = lax.axis_index(axis)

    def entry(k):
        return lax.dynamic_index_in_dim(block, lax.rem(me + 4 - k, 4), dim, keepdims=False)

    return [entry(0)] + [shift(entry(k), axis, -k) for k in (1, 2, 3)]


def after(array, *others):
    return lax.optimization_barrier((array, *others))[0]


def collect_tokens(*arrays):
    count = len(arrays)
    block = jnp.stack([a.reshape(2, 16, 4, 2, 256) for a in arrays], 0)
    block = block.transpose(3, 1, 0, 2, 4, 5).reshape(8, count, 16, 2, 256)
    block = lax.all_to_all(block, ("zh", "c"), 0, 0, tiled=True)
    block = block.reshape(4, 2, count, 16, 2, 256).transpose(2, 0, 3, 4, 1, 5)
    return block.reshape(count, 64, 1024)


def spread_tokens(*arrays):
    block = jnp.stack([a.reshape(4, 16, 2, 2, 256) for a in arrays], 0)
    block = block.transpose(1, 4, 0, 2, 3, 5).reshape(8, len(arrays), 16, 2, 256)
    block = lax.all_to_all(block, ("zh", "c"), 0, 0, tiled=True)
    block = block.reshape(4, 2, len(arrays), 16, 2, 256).transpose(2, 1, 3, 0, 4, 5)
    return block.reshape(len(arrays), 32, 2048)


def local(tokens, gate_weight, up_weight, down_weight, out_cotangent):
    z = (lax.axis_index("zh") * 2 + lax.axis_index("zl")).astype(jnp.int32)
    width = gate_weight.shape[1]

    rows = lax.all_gather(jnp.concatenate([gate_weight, up_weight], 1), Z, axis=0, tiled=True)
    down_cols = ring_gather_z(down_weight, z)
    inputs, cotangent = gather_tokens(spread_tokens(tokens, out_cotangent))

    hidden_grad = core_sum(product(cotangent, down_cols, 1, 1))
    total = core_sum(product(inputs, rows, 1, 0))
    gate, up_value = total[:, :width], total[:, width:]
    activation, slope = gelu_pair(gate)
    hidden = (activation * up_value).astype(BF16)
    grads = jnp.concatenate(
        [(hidden_grad * up_value * slope).astype(BF16), (hidden_grad * activation).astype(BF16)], 1
    )
    ring = ring_scatter_z(product(hidden, cotangent, 0, 0), z)
    pair = next(ring)
    weight_partial = product(inputs, after(grads, *pair), 0, 0)
    weight_grads = lax.psum_scatter(weight_partial, Z, scatter_dimension=0, tiled=True)
    output = product(after(hidden, weight_partial), down_cols, 1, 0).reshape(4, 4, 32, -1)
    output = scatter_start(output, "x", 1)
    input_grad = product(after(grads, weight_partial), rows, 1, 1).reshape(4, 4, 32, -1)
    input_grad = lax.all_to_all(input_grad, "y", 0, 0, tiled=True)
    pair = ring.send(pair)
    output = add(*scatter_start(add(after(output[0], *pair), *output[1:]), "y"))
    input_grad = input_grad.astype(F32).sum(0).astype(BF16)
    input_grad = add(*scatter_start(input_grad, "x"))
    for _ in range(2):
        pair = ring.send(pair)
    down_weight_grad = ring.send(pair)
    output, input_grad = collect_tokens(output, input_grad)
    return (output, input_grad, weight_grads[:, :width], weight_grads[:, width:], down_weight_grad)


def solution(mesh):
    fine = Mesh(mesh.devices.reshape(4, 4, 4, 2, 2), ("x", "y", "zh", "zl", "c"))
    token_spec = P(("zl", "c", "x", "y"), "zh")
    in_spec = P(("zh", "zl", "c"), ("x", "y"))
    out_spec = P(("x", "y"), ("zh", "zl", "c"))
    return jax.shard_map(
        local,
        mesh=fine,
        in_specs=(token_spec, in_spec, in_spec, out_spec, token_spec),
        out_specs=(token_spec, token_spec, in_spec, in_spec, out_spec),
        check_vma=False,
    )
```

```python
import math

import jax
import jax.numpy as jnp
from jax import lax
from jax.sharding import Mesh
from jax.sharding import PartitionSpec as P

gelu_scale = math.sqrt(2.0 / math.pi)
cubic_coef = 0.044715
F32, BF16 = jnp.float32, jnp.bfloat16
Z = ("zh", "zl")
NZ = 8


def gelu_pair(value):
    inner = gelu_scale * (value + cubic_coef * value * value * value)
    tangent = jnp.tanh(inner)
    activation = 0.5 * value * (1.0 + tangent)
    slope = 0.5 * (1.0 + tangent) + 0.5 * value * (1.0 - tangent * tangent) * gelu_scale * (
        1.0 + 3.0 * cubic_coef * value * value
    )
    return (activation, slope)


def product(left, right, left_dim, right_dim):
    return lax.dot_general(
        left, right, (((left_dim,), (right_dim,)), ((), ())), preferred_element_type=F32
    ).astype(BF16)


def shift(array, axis, by, size=4):
    return lax.ppermute(array, axis, [(i, (i + by) % size) for i in range(size)])


def add(*terms):
    return sum(t.astype(F32) for t in terms).astype(BF16)


def core_sum(part):
    return part.astype(F32) + shift(part, "c", 1, 2).astype(F32)


def ring_scatter_z(partial, z):
    rows, columns = partial.shape[0], partial.shape[1] // NZ
    half = rows // 2

    def take(ahead, offset=0, count=rows):
        start = (jnp.int32(offset), lax.rem(z + ahead, NZ) * columns)
        return lax.dynamic_slice(partial, start, (count, columns))

    def send(pair):
        return shift(pair[0], Z, 1, NZ), shift(pair[1], Z, -1, NZ)

    up, down = send((yield take(4, 0, half), take(4, half, half)))
    up = jnp.concatenate([add(take(3, 0, half), up), take(3, half, half)], 0)
    down = jnp.concatenate([take(5, 0, half), add(take(5, half, half), down)], 0)
    up, down = lax.optimization_barrier((up, down))
    for step in (2, 1):
        up, down = send((yield up, down))
        up, down = lax.optimization_barrier((add(take(step), up), add(take(NZ - step), down)))
    up, down = send((yield up, down))
    yield add(take(0), up, down)


def ring_gather_z(block, z):
    rows, columns = block.shape
    half = rows // 2
    out = jnp.zeros((rows, NZ * columns), block.dtype)

    def put(out, piece, back, offset=0):
        start = (jnp.int32(offset), lax.rem(z + NZ - back, NZ) * columns)
        return lax.dynamic_update_slice(out, piece, start)

    out = put(out, block, 0)
    back = ahead = block
    for step in (1, 2, 3):
        back, ahead = shift(back, Z, 1, NZ), shift(ahead, Z, -1, NZ)
        out = put(put(out, back, step), ahead, NZ - step)
    out = put(out, shift(back[:half], Z, 1, NZ), 4)
    return put(out, shift(ahead[half:], Z, -1, NZ), 4, half)


def put(out, piece, dim, at, offset=0):
    start = [jnp.int32(0)] * out.ndim
    start[1 - dim], start[dim] = jnp.int32(offset), at
    return lax.dynamic_update_slice(out, jnp.expand_dims(piece, dim), start)


def gather_four(block, axis):
    me = lax.axis_index(axis)
    out = jnp.zeros((4,) + block.shape, block.dtype)
    for k in range(4):
        out = put(out, shift(block, axis, k) if k else block, 0, lax.rem(me + 4 - k, 4))
    return out


def gather_tokens(tokens, cotangent):
    inner, other = gather_four(tokens, "x"), gather_four(cotangent, "y")
    back, ahead = shift(inner, "y", 1), shift(inner, "y", -1)
    other = lax.all_to_all(jnp.broadcast_to(other[None], (4,) + other.shape), "x", 0, 0, tiled=True)
    y = lax.axis_index("y")
    out = jnp.zeros((4,) + inner.shape, inner.dtype)
    for k, piece in ((0, inner), (1, back), (3, ahead)):
        out = put(out, piece, 1, lax.rem(y + 4 - k, 4))
    for offset, piece in ((0, shift(back[:2], "y", 1)), (2, shift(ahead[2:], "y", -1))):
        out = put(out, piece, 1, lax.rem(y + 2, 4), offset)
    return out.reshape(512, -1), other.reshape(512, -1)


def scatter_start(block, axis, dim=0):
    me = lax.axis_index(axis)

    def entry(k):
        return lax.dynamic_index_in_dim(block, lax.rem(me + 4 - k, 4), dim, keepdims=False)

    return [entry(0)] + [shift(entry(k), axis, -k) for k in (1, 2, 3)]


def after(array, *others):
    return lax.optimization_barrier((array, *others))[0]


def collect_tokens(*arrays):
    count = len(arrays)
    block = jnp.stack([a.reshape(2, 16, 4, 2, 256) for a in arrays], 0)
    block = block.transpose(3, 1, 0, 2, 4, 5).reshape(8, count, 16, 2, 256)
    block = lax.all_to_all(block, ("zh", "c"), 0, 0, tiled=True)
    block = block.reshape(4, 2, count, 16, 2, 256).transpose(2, 0, 3, 4, 1, 5)
    return block.reshape(count, 64, 1024)


def spread_tokens(*arrays):
    block = jnp.stack([a.reshape(4, 16, 2, 2, 256) for a in arrays], 0)
    block = block.transpose(1, 4, 0, 2, 3, 5).reshape(8, len(arrays), 16, 2, 256)
    block = lax.all_to_all(block, ("zh", "c"), 0, 0, tiled=True)
    block = block.reshape(4, 2, len(arrays), 16, 2, 256).transpose(2, 1, 3, 0, 4, 5)
    return block.reshape(len(arrays), 32, 2048)


def local(tokens, gate_weight, up_weight, down_weight, out_cotangent):
    z = (lax.axis_index("zh") * 2 + lax.axis_index("zl")).astype(jnp.int32)
    width = gate_weight.shape[1]

    rows = lax.all_gather(jnp.concatenate([gate_weight, up_weight], 1), Z, axis=0, tiled=True)
    down_cols = ring_gather_z(down_weight, z)
    inputs, cotangent = gather_tokens(*spread_tokens(tokens, out_cotangent))

    hidden_grad = product(cotangent, down_cols, 1, 1)
    total = core_sum(product(after(inputs, hidden_grad), rows, 1, 0))
    hidden_grad = core_sum(hidden_grad)
    gate, up_value = total[:, :width], total[:, width:]
    activation, slope = gelu_pair(gate)
    hidden = (activation * up_value).astype(BF16)
    grads = jnp.concatenate(
        [(hidden_grad * up_value * slope).astype(BF16), (hidden_grad * activation).astype(BF16)], 1
    )
    weight_partial = product(inputs, grads, 0, 0)
    weight_grads = lax.psum_scatter(weight_partial, Z, scatter_dimension=0, tiled=True)
    hidden = after(hidden, weight_partial)
    ring = ring_scatter_z(product(hidden, cotangent, 0, 0), z)
    pair = next(ring)
    output = product(after(hidden, *pair), down_cols, 1, 0).reshape(4, 4, 32, -1)
    output = scatter_start(output, "y", 1)
    input_grad = product(after(grads, *pair), rows, 1, 1).reshape(4, 4, 32, -1)
    input_grad = lax.all_to_all(input_grad, "x", 0, 0, tiled=True)
    pair = ring.send(pair)
    output = add(*scatter_start(add(after(output[0], *pair), *output[1:]), "x"))
    input_grad = input_grad.astype(F32).sum(0).astype(BF16)
    input_grad = add(*scatter_start(input_grad, "y"))
    for _ in range(2):
        pair = ring.send(pair)
    down_weight_grad = ring.send(pair)
    output, input_grad = collect_tokens(output, input_grad)
    return (output, input_grad, weight_grads[:, :width], weight_grads[:, width:], down_weight_grad)


def solution(mesh):
    fine = Mesh(mesh.devices.reshape(4, 4, 4, 2, 2), ("x", "y", "zh", "zl", "c"))
    token_spec = P(("zl", "c", "x", "y"), "zh")
    in_spec = P(("zh", "zl", "c"), ("x", "y"))
    out_spec = P(("x", "y"), ("zh", "zl", "c"))
    return jax.shard_map(
        local,
        mesh=fine,
        in_specs=(token_spec, in_spec, in_spec, out_spec, token_spec),
        out_specs=(token_spec, token_spec, in_spec, in_spec, out_spec),
        check_vma=False,
    )
```

```python
import math

import jax
import jax.numpy as jnp
from jax import lax
from jax.sharding import Mesh
from jax.sharding import PartitionSpec as P

gelu_scale = math.sqrt(2.0 / math.pi)
cubic_coef = 0.044715
F32, BF16 = jnp.float32, jnp.bfloat16
Z = ("zh", "zl")
NZ = 8


def gelu_pair(value):
    inner = gelu_scale * (value + cubic_coef * value * value * value)
    tangent = jnp.tanh(inner)
    activation = 0.5 * value * (1.0 + tangent)
    slope = 0.5 * (1.0 + tangent) + 0.5 * value * (1.0 - tangent * tangent) * gelu_scale * (
        1.0 + 3.0 * cubic_coef * value * value
    )
    return (activation, slope)


def product(left, right, left_dim, right_dim):
    return lax.dot_general(
        left, right, (((left_dim,), (right_dim,)), ((), ())), preferred_element_type=F32
    ).astype(BF16)


def shift(array, axis, by, size=4):
    return lax.ppermute(array, axis, [(i, (i + by) % size) for i in range(size)])


def add(*terms):
    return sum(t.astype(F32) for t in terms).astype(BF16)


def core_sum(part):
    return part.astype(F32) + shift(part, "c", 1, 2).astype(F32)


def ring_scatter_z(partial, z):
    rows, columns = partial.shape[0], partial.shape[1] // NZ
    half = rows // 2

    def take(ahead, offset=0, count=rows):
        start = (jnp.int32(offset), lax.rem(z + ahead, NZ) * columns)
        return lax.dynamic_slice(partial, start, (count, columns))

    def send(pair):
        return shift(pair[0], Z, 1, NZ), shift(pair[1], Z, -1, NZ)

    up, down = send((yield take(4, 0, half), take(4, half, half)))
    up = jnp.concatenate([add(take(3, 0, half), up), take(3, half, half)], 0)
    down = jnp.concatenate([take(5, 0, half), add(take(5, half, half), down)], 0)
    up, down = lax.optimization_barrier((up, down))
    for step in (2, 1):
        up, down = send((yield up, down))
        up, down = lax.optimization_barrier((add(take(step), up), add(take(NZ - step), down)))
    up, down = send((yield up, down))
    yield add(take(0), up, down)


def ring_gather_z(block, z):
    rows, columns = block.shape
    half = rows // 2
    out = jnp.zeros((rows, NZ * columns), block.dtype)

    def put(out, piece, back, offset=0):
        start = (jnp.int32(offset), lax.rem(z + NZ - back, NZ) * columns)
        return lax.dynamic_update_slice(out, piece, start)

    out = put(out, block, 0)
    back = ahead = block
    for step in (1, 2, 3):
        back, ahead = shift(back, Z, 1, NZ), shift(ahead, Z, -1, NZ)
        out = put(put(out, back, step), ahead, NZ - step)
    out = put(out, shift(back[:half], Z, 1, NZ), 4)
    return put(out, shift(ahead[half:], Z, -1, NZ), 4, half)


def put(out, piece, dim, at, offset=0):
    start = [jnp.int32(0)] * out.ndim
    start[1 - dim], start[dim] = jnp.int32(offset), at
    return lax.dynamic_update_slice(out, jnp.expand_dims(piece, dim), start)


def gather_four(block, axis):
    me = lax.axis_index(axis)
    out = jnp.zeros((4,) + block.shape, block.dtype)
    for k in range(4):
        out = put(out, shift(block, axis, k) if k else block, 0, lax.rem(me + 4 - k, 4))
    return out


def gather_tokens(tokens, cotangent):
    inner, other = gather_four(tokens, "x"), gather_four(cotangent, "y")
    back, ahead = shift(inner, "y", 1), shift(inner, "y", -1)
    other = lax.all_to_all(jnp.broadcast_to(other[None], (4,) + other.shape), "x", 0, 0, tiled=True)
    y = lax.axis_index("y")
    out = jnp.zeros((4,) + inner.shape, inner.dtype)
    for k, piece in ((0, inner), (1, back), (3, ahead)):
        out = put(out, piece, 1, lax.rem(y + 4 - k, 4))
    for offset, piece in ((0, shift(back[:2], "y", 1)), (2, shift(ahead[2:], "y", -1))):
        out = put(out, piece, 1, lax.rem(y + 2, 4), offset)
    return out.reshape(512, -1), other.reshape(512, -1)


def scatter_start(block, axis, dim=0):
    me = lax.axis_index(axis)

    def entry(k):
        return lax.dynamic_index_in_dim(block, lax.rem(me + 4 - k, 4), dim, keepdims=False)

    return [entry(0)] + [shift(entry(k), axis, -k) for k in (1, 2, 3)]


def after(array, *others):
    return lax.optimization_barrier((array, *others))[0]


def collect_tokens(arrays, others):
    count = len(arrays)
    block = jnp.stack([a.reshape(2, 16, 4, 2, 256) for a in arrays], 0)
    block = block.transpose(3, 1, 0, 2, 4, 5).reshape(8, count, 16, 2, 256)
    block = after(lax.all_to_all(block, ("zh", "c"), 0, 0, tiled=True), *others)
    block = block.reshape(4, 2, count, 16, 2, 256).transpose(2, 0, 3, 4, 1, 5)
    return block.reshape(count, 64, 1024)


def spread_tokens(*arrays):
    block = jnp.stack([a.reshape(4, 16, 2, 2, 256) for a in arrays], 0)
    block = block.transpose(1, 4, 0, 2, 3, 5).reshape(8, len(arrays), 16, 2, 256)
    block = lax.all_to_all(block, ("zh", "c"), 0, 0, tiled=True)
    block = block.reshape(4, 2, len(arrays), 16, 2, 256).transpose(2, 1, 3, 0, 4, 5)
    return block.reshape(len(arrays), 32, 2048)


def local(tokens, gate_weight, up_weight, down_weight, out_cotangent):
    z = (lax.axis_index("zh") * 2 + lax.axis_index("zl")).astype(jnp.int32)
    width = gate_weight.shape[1]

    rows = lax.all_gather(jnp.concatenate([gate_weight, up_weight], 1), Z, axis=0, tiled=True)
    down_cols = ring_gather_z(down_weight, z)
    inputs, cotangent = gather_tokens(*spread_tokens(tokens, out_cotangent))

    hidden_grad = product(cotangent, down_cols, 1, 1)
    total = core_sum(product(after(inputs, hidden_grad), rows, 1, 0))
    hidden_grad = core_sum(hidden_grad)
    gate, up_value = total[:, :width], total[:, width:]
    activation, slope = gelu_pair(gate)
    hidden = (activation * up_value).astype(BF16)
    grads = jnp.concatenate(
        [(hidden_grad * up_value * slope).astype(BF16), (hidden_grad * activation).astype(BF16)], 1
    )
    weight_partial = product(inputs, grads, 0, 0)
    weight_grads = lax.psum_scatter(weight_partial, Z, scatter_dimension=0, tiled=True)
    hidden = after(hidden, weight_partial)
    ring = ring_scatter_z(product(hidden, cotangent, 0, 0), z)
    pair = next(ring)
    output = product(after(hidden, *pair), down_cols, 1, 0).reshape(4, 4, 32, -1)
    output = scatter_start(output, "y", 1)
    input_grad = product(after(grads, *pair), rows, 1, 1).reshape(4, 4, 32, -1)
    input_grad = lax.all_to_all(input_grad, "x", 0, 0, tiled=True)
    pair = ring.send(pair)
    output = add(*scatter_start(add(after(output[0], *pair), *output[1:]), "x"))
    input_grad = input_grad.astype(F32).sum(0).astype(BF16)
    input_grad = add(*scatter_start(input_grad, "y"))
    for _ in range(2):
        pair = ring.send(pair)
    down_weight_grad = ring.send(pair)
    gate_weight_grad, up_weight_grad = weight_grads[:, :width], weight_grads[:, width:]
    output, input_grad = collect_tokens((output, input_grad), (gate_weight_grad, up_weight_grad))
    return (output, input_grad, gate_weight_grad, up_weight_grad, down_weight_grad)


def solution(mesh):
    fine = Mesh(mesh.devices.reshape(4, 4, 4, 2, 2), ("x", "y", "zh", "zl", "c"))
    token_spec = P(("zl", "c", "x", "y"), "zh")
    in_spec = P(("zh", "zl", "c"), ("x", "y"))
    out_spec = P(("x", "y"), ("zh", "zl", "c"))
    return jax.shard_map(
        local,
        mesh=fine,
        in_specs=(token_spec, in_spec, in_spec, out_spec, token_spec),
        out_specs=(token_spec, token_spec, in_spec, in_spec, out_spec),
        check_vma=False,
    )
```

```python
import math

import jax
import jax.numpy as jnp
from jax import lax
from jax.sharding import Mesh
from jax.sharding import PartitionSpec as P

gelu_scale = math.sqrt(2.0 / math.pi)
cubic_coef = 0.044715
F32, BF16 = jnp.float32, jnp.bfloat16
Z = ("zh", "zl")
NZ = 8


def gelu_pair(value):
    inner = gelu_scale * (value + cubic_coef * value * value * value)
    tangent = jnp.tanh(inner)
    activation = 0.5 * value * (1.0 + tangent)
    slope = 0.5 * (1.0 + tangent) + 0.5 * value * (1.0 - tangent * tangent) * gelu_scale * (
        1.0 + 3.0 * cubic_coef * value * value
    )
    return (activation, slope)


def product(left, right, left_dim, right_dim):
    return lax.dot_general(
        left, right, (((left_dim,), (right_dim,)), ((), ())), preferred_element_type=F32
    ).astype(BF16)


def shift(array, axis, by, size=4):
    return lax.ppermute(array, axis, [(i, (i + by) % size) for i in range(size)])


def add(*terms):
    return sum(t.astype(F32) for t in terms).astype(BF16)


def core_sum(part):
    return part.astype(F32) + shift(part, "c", 1, 2).astype(F32)


def ring_scatter_z(partial, z):
    rows, columns = partial.shape[0], partial.shape[1] // NZ
    half = rows // 2

    def take(ahead, offset=0, count=rows):
        start = (jnp.int32(offset), lax.rem(z + ahead, NZ) * columns)
        return lax.dynamic_slice(partial, start, (count, columns))

    def send(pair):
        return shift(pair[0], Z, 1, NZ), shift(pair[1], Z, -1, NZ)

    up, down = send((yield take(4, 0, half), take(4, half, half)))
    up = jnp.concatenate([add(take(3, 0, half), up), take(3, half, half)], 0)
    down = jnp.concatenate([take(5, 0, half), add(take(5, half, half), down)], 0)
    up, down = lax.optimization_barrier((up, down))
    for step in (2, 1):
        up, down = send((yield up, down))
        up, down = lax.optimization_barrier((add(take(step), up), add(take(NZ - step), down)))
    up, down = send((yield up, down))
    yield add(take(0), up, down)


def ring_gather_z(block, z):
    rows, columns = block.shape
    half = rows // 2
    out = jnp.zeros((rows, NZ * columns), block.dtype)

    def put(out, piece, back, offset=0):
        start = (jnp.int32(offset), lax.rem(z + NZ - back, NZ) * columns)
        return lax.dynamic_update_slice(out, piece, start)

    out = put(out, block, 0)
    back = ahead = block
    for step in (1, 2, 3):
        back, ahead = shift(back, Z, 1, NZ), shift(ahead, Z, -1, NZ)
        out = put(put(out, back, step), ahead, NZ - step)
    out = put(out, shift(back[:half], Z, 1, NZ), 4)
    return put(out, shift(ahead[half:], Z, -1, NZ), 4, half)


def put(out, piece, dim, at, offset=0):
    start = [jnp.int32(0)] * out.ndim
    start[1 - dim], start[dim] = jnp.int32(offset), at
    return lax.dynamic_update_slice(out, jnp.expand_dims(piece, dim), start)


def gather_four(block, axis):
    me = lax.axis_index(axis)
    out = jnp.zeros((4,) + block.shape, block.dtype)
    for k in range(4):
        out = put(out, shift(block, axis, k) if k else block, 0, lax.rem(me + 4 - k, 4))
    return out


def gather_tokens(tokens, cotangent):
    inner, other = gather_four(tokens, "x"), gather_four(cotangent, "y")
    back, ahead = shift(inner, "y", 1), shift(inner, "y", -1)
    other = lax.all_to_all(jnp.broadcast_to(other[None], (4,) + other.shape), "x", 0, 0, tiled=True)
    y = lax.axis_index("y")
    out = jnp.zeros((4,) + inner.shape, inner.dtype)
    for k, piece in ((0, inner), (1, back), (3, ahead)):
        out = put(out, piece, 1, lax.rem(y + 4 - k, 4))
    for offset, piece in ((0, shift(back[:2], "y", 1)), (2, shift(ahead[2:], "y", -1))):
        out = put(out, piece, 1, lax.rem(y + 2, 4), offset)
    return out.reshape(512, -1), other.reshape(512, -1)


def scatter_start(block, axis, dim=0):
    me = lax.axis_index(axis)

    def entry(k):
        return lax.dynamic_index_in_dim(block, lax.rem(me + 4 - k, 4), dim, keepdims=False)

    return [entry(0)] + [shift(entry(k), axis, -k) for k in (1, 2, 3)]


def after(array, *others):
    return lax.optimization_barrier((array, *others))[0]


def collect_tokens(arrays, others):
    count = len(arrays)
    block = jnp.stack([a.reshape(2, 16, 4, 2, 256) for a in arrays], 0)
    block = block.transpose(3, 1, 0, 2, 4, 5).reshape(8, count, 16, 2, 256)
    block = after(lax.all_to_all(block, ("zh", "c"), 0, 0, tiled=True), *others)
    block = block.reshape(4, 2, count, 16, 2, 256).transpose(2, 0, 3, 4, 1, 5)
    return block.reshape(count, 64, 1024)


def spread_tokens(*arrays):
    block = jnp.stack([a.reshape(4, 16, 2, 2, 256) for a in arrays], 0)
    block = block.transpose(1, 4, 0, 2, 3, 5).reshape(8, len(arrays), 16, 2, 256)
    block = lax.all_to_all(block, ("zh", "c"), 0, 0, tiled=True)
    block = block.reshape(4, 2, len(arrays), 16, 2, 256).transpose(2, 1, 3, 0, 4, 5)
    return block.reshape(len(arrays), 32, 2048)


def local(tokens, gate_weight, up_weight, down_weight, out_cotangent):
    z = (lax.axis_index("zh") * 2 + lax.axis_index("zl")).astype(jnp.int32)
    width = gate_weight.shape[1]

    rows = lax.all_gather(jnp.concatenate([gate_weight, up_weight], 1), Z, axis=0, tiled=True)
    down_cols = ring_gather_z(down_weight, z)
    inputs, cotangent = gather_tokens(*spread_tokens(tokens, out_cotangent))

    hidden_grad = product(cotangent, down_cols, 1, 1)
    total = core_sum(product(after(inputs, hidden_grad), rows, 1, 0))
    hidden_grad = core_sum(hidden_grad)
    gate, up_value = total[:, :width], total[:, width:]
    activation, slope = gelu_pair(gate)
    hidden = (activation * up_value).astype(BF16)
    grads = jnp.concatenate(
        [(hidden_grad * up_value * slope).astype(BF16), (hidden_grad * activation).astype(BF16)], 1
    )
    weight_partial = product(inputs, grads, 0, 0)
    weight_grads = lax.psum_scatter(weight_partial, Z, scatter_dimension=0, tiled=True)
    hidden = after(hidden, weight_partial)
    ring = ring_scatter_z(product(hidden, cotangent, 0, 0), z)
    pair = next(ring)
    output = product(after(hidden, *pair), down_cols, 1, 0).reshape(4, 4, 32, -1)
    output = scatter_start(output, "y", 1)
    input_grad = product(after(grads, *pair), rows, 1, 1).reshape(4, 4, 32, -1)
    input_grad = lax.all_to_all(input_grad, "x", 0, 0, tiled=True)
    pair = ring.send(pair)
    output = add(*scatter_start(add(after(output[0], *pair), *output[1:]), "x"))
    input_grad = input_grad.astype(F32).sum(0).astype(BF16)
    input_grad = add(*scatter_start(input_grad, "y"))
    for _ in range(2):
        pair = ring.send(pair)
    down_weight_grad = ring.send([after(p, output, input_grad) for p in pair])
    gate_weight_grad, up_weight_grad = weight_grads[:, :width], weight_grads[:, width:]
    output, input_grad = collect_tokens((output, input_grad), (gate_weight_grad, up_weight_grad))
    return (output, input_grad, gate_weight_grad, up_weight_grad, down_weight_grad)


def solution(mesh):
    fine = Mesh(mesh.devices.reshape(4, 4, 4, 2, 2), ("x", "y", "zh", "zl", "c"))
    token_spec = P(("zl", "c", "x", "y"), "zh")
    in_spec = P(("zh", "zl", "c"), ("x", "y"))
    out_spec = P(("x", "y"), ("zh", "zl", "c"))
    return jax.shard_map(
        local,
        mesh=fine,
        in_specs=(token_spec, in_spec, in_spec, out_spec, token_spec),
        out_specs=(token_spec, token_spec, in_spec, in_spec, out_spec),
        check_vma=False,
    )
```
